32 devices in a mesh: req: 16 (over z, x, core), tp: 2 (over y).
Axes of the slice: x: 2, y: 2, z: 4, core: 2. Of those that a mesh axis runs over, the one named last changes fastest.
Arguments:
- q_new: bfloat16 [1024, 5120], P('req', 'tp'), may hold values from -6 to 6
- k_new: bfloat16 [1024, 1024], P('req', 'tp'), may hold values from -15 to 15
- v_new: bfloat16 [1024, 1024], P('req', 'tp'), may hold values from -6 to 6
- k_cache: bfloat16 [256, 128, 1024], P('req', None, 'tp'), may hold values from -16 to 16
- v_cache: bfloat16 [256, 128, 1024], P('req', None, 'tp'), may hold values from -6 to 6
- lengths: int32 [8], replicated, may hold values from 1 to 4096, as said below
- page_table: int32 [8, 32], replicated, may hold values from -1 to 255, as said below
- w_out: bfloat16 [5120, 5120], P('req', 'tp'), may hold values from -0.078125 to 0.078125
Outputs:
- attn_out: bfloat16 [1024, 5120], P('req')
The draws below stay inside these ranges and needn't reach their ends.
Inputs may be any that keep to these rules, and one draw needn't show every extreme that they name: `lengths`: the last request, 7, has exactly 4096 cached tokens; every request has at least one. `page_table`: request r uses ceil(lengths[r] / 128) logical pages. Its first ceil(ceil(lengths[r] / 128) / 2) logical pages lie among global pages 2r * 16 to (2r + 1) * 16 - 1, the rest among (2r + 1) * 16 to (2r + 2) * 16 - 1; distinct logical pages use distinct global pages; entries past a request's last page are -1.
All inputs are finite; a program needn't handle non-finite values.
Results may differ from the reference program's by a relative error of at most 0.024.
Values may be sent and summed in bfloat16 or wider, within the bound.
A program may use at most 128 MiB of HBM per device.

```python
import math
import jax
import jax.numpy as jnp
from jax import lax

D = 5120
QH = 40
KVH = 8
HD = 128
GROUP = 5
NEW = 128
PAGE = 128
PAGES_DEV = 16
REQS = 8
TOKENS = 1024
LMAX = 4096
MAXP = 32
POOL = 256
N_REQ = 16


def lengths_common(key):
    first_key = jax.random.fold_in(key, 7)
    drawn = jax.random.randint(first_key, (REQS,), 1, LMAX + 1)
    return jnp.where(jnp.arange(REQS) == REQS - 1, LMAX, drawn).astype(jnp.int32)


def draw_lengths(key, part):
    return lengths_common(key)


def draw_page_table(key, part):
    lengths = lengths_common(key)
    page_count = (lengths + PAGE - 1) // PAGE
    even_pages = (page_count + 1) // 2
    logical = jnp.arange(MAXP)
    row_keys = jax.random.split(jax.random.fold_in(key, 13), N_REQ)
    orders = jax.vmap(lambda one_key: jax.random.permutation(one_key, PAGES_DEV))(row_keys)
    on_odd = logical[None, :] >= even_pages[:, None]
    device_row = 2 * jnp.arange(REQS)[:, None] + on_odd.astype(jnp.int32)
    position = jnp.where(on_odd, logical[None, :] - even_pages[:, None], logical[None, :])
    position = jnp.clip(position, 0, PAGES_DEV - 1)
    slot = orders[device_row, position]
    global_page = device_row * PAGES_DEV + slot
    return jnp.where(logical[None, :] < page_count[:, None], global_page, -1).astype(jnp.int32)


def draw_q_new(key, part):
    base_key = jax.random.fold_in(key, 21)
    drawn = jnp.clip(jax.random.normal(base_key, (TOKENS, QH * HD), jnp.float32), -6.0, 6.0)
    return drawn.astype(jnp.bfloat16)


def draw_k_new(key, part):
    base_key = jax.random.fold_in(key, 23)
    drawn = jnp.clip(2.5 * jax.random.normal(base_key, (TOKENS, KVH * HD), jnp.float32), -15.0, 15.0)
    return drawn.astype(jnp.bfloat16)


def level_of(own_key, dims, pieces, smallest, high):
    def one(dim, shards_of):
        steps = jax.random.uniform(jax.random.fold_in(jax.random.fold_in(own_key, 6), dim), (shards_of,), jnp.float32, smallest / len(pieces), high / len(pieces))
        return jnp.repeat(jnp.exp(steps), dims[dim] // shards_of).reshape((-1,) + (1,) * (len(dims) - dim - 1))

    level = one(*pieces[0])
    for cut in pieces[1:]:
        level = level * one(*cut)
    return level


def bell_draw(stream_key, shape, width, reach, cuts=(), kind=jnp.bfloat16):
    factor_of = level_of(stream_key, shape, cuts, -0.22, 0.18) if cuts else 1.0
    entries = jax.random.normal(stream_key, shape, jnp.float32) * width * factor_of
    return jnp.minimum(jnp.maximum(entries, -reach), reach).astype(kind)


def setup_inputs(seed: int = 0) -> dict:
    streams_of = jax.random.split(jax.random.key(seed), 9)
    q_new = draw_q_new(jax.random.fold_in(streams_of[8], 71), 0)
    k_new = draw_k_new(jax.random.fold_in(streams_of[8], 71), 0)
    v_new = bell_draw(streams_of[2], (TOKENS, KVH * HD), 1.0, 6.0, ((0, 16), (1, 2)))
    k_cache = bell_draw(streams_of[3], (POOL, PAGE, KVH * HD), 2.5, 16.0, ((0, 16), (2, 2)))
    v_cache = bell_draw(streams_of[4], (POOL, PAGE, KVH * HD), 1.0, 6.0, ((0, 16), (2, 2)))
    lengths = draw_lengths(jax.random.fold_in(streams_of[8], 71), 0)
    page_table = draw_page_table(jax.random.fold_in(streams_of[8], 71), 0)
    w_out = bell_draw(streams_of[7], (D, QH * HD), (QH * HD) ** -0.5, 0.078125, ((0, 16), (1, 2)))
    return dict(q_new=q_new, k_new=k_new, v_new=v_new, k_cache=k_cache, v_cache=v_cache, lengths=lengths, page_table=page_table, w_out=w_out)


ROPE_BASE = 1000000.0

def rotate(values, places):
    inverse = 1.0 / ROPE_BASE ** (jnp.arange(0, HD, 2).astype(jnp.float32) / HD)
    angles = places.astype(jnp.float32)[:, None] * inverse[None, :]
    cosine = jnp.concatenate([jnp.cos(angles), jnp.cos(angles)], axis=-1)[:, None, :]
    sine = jnp.concatenate([jnp.sin(angles), jnp.sin(angles)], axis=-1)[:, None, :]
    first_half = values[..., :HD // 2]
    second_half = values[..., HD // 2:]
    turned = jnp.concatenate([-second_half, first_half], axis=-1)
    return values * cosine + turned * sine

def reference(q_new, k_new, v_new, k_cache, v_cache, lengths, page_table, w_out):
    scale = 1.0 / math.sqrt(HD)
    queries = q_new.reshape(REQS, NEW, QH, HD)
    fresh_keys = k_new.reshape(REQS, NEW, KVH, HD)
    fresh_values = v_new.reshape(REQS, NEW, KVH, HD)
    pool_keys = k_cache.reshape(POOL, PAGE, KVH, HD)
    pool_values = v_cache.reshape(POOL, PAGE, KVH, HD)

    def one_request(items):
        query, key_new, value_new, length, table_row = items
        places = length + jnp.arange(NEW).astype(jnp.int32)
        query_rot = rotate(query.astype(jnp.float32), places).astype(jnp.bfloat16)
        query_rot = query_rot.reshape(NEW, KVH, GROUP, HD)
        key_rot = rotate(key_new.astype(jnp.float32), places).astype(jnp.bfloat16)
        slots = jnp.clip(table_row, 0, POOL - 1)
        cached_keys = pool_keys[slots].reshape(MAXP * PAGE, KVH, HD)
        cached_values = pool_values[slots].reshape(MAXP * PAGE, KVH, HD)
        all_keys = jnp.concatenate([cached_keys, key_rot], axis=0)
        all_values = jnp.concatenate([cached_values, value_new], axis=0)
        cache_index = jnp.arange(MAXP * PAGE).astype(jnp.int32)
        key_places = jnp.concatenate([cache_index, places])
        usable = jnp.concatenate([cache_index < length, jnp.ones((NEW,), bool)])
        allowed = usable[None, :] & (key_places[None, :] <= places[:, None])

        def one_head(head_items):
            head_query, head_keys, head_values = head_items
            scores = jnp.einsum('qgd,kd->gqk', head_query.astype(jnp.float32), head_keys.astype(jnp.float32)) * scale
            scores = jnp.where(allowed[None], scores, -jnp.inf)
            highest = lax.optimization_barrier(jnp.max(scores, axis=-1, keepdims=True))
            weights = jnp.exp(scores - highest)
            total = lax.optimization_barrier(jnp.sum(weights, axis=-1))
            rounded = lax.optimization_barrier(weights.astype(jnp.bfloat16))
            mixed = jnp.einsum('gqk,kd->qgd', rounded.astype(jnp.float32), head_values.astype(jnp.float32))
            return mixed / jnp.transpose(total)[..., None]
        heads = lax.map(one_head, (jnp.moveaxis(query_rot, 1, 0), jnp.moveaxis(all_keys, 1, 0), jnp.moveaxis(all_values, 1, 0)))
        return jnp.moveaxis(heads, 0, 1).reshape(NEW, QH * HD).astype(jnp.bfloat16)
    attention = lax.map(one_request, (queries, fresh_keys, fresh_values, lengths, page_table))
    attention = attention.reshape(TOKENS, QH * HD)
    return jnp.dot(attention, w_out.T, preferred_element_type=jnp.float32).astype(jnp.bfloat16)
```

```python
import math

import jax
import jax.numpy as jnp
from jax import lax
from jax.experimental import pallas as pl
from jax.experimental.pallas import tpu as pltpu
from jax.sharding import PartitionSpec as P

HD = 128
GROUP = 5
CHUNK = 512
ROPE_BASE = 1000000.0
FLOOR_SCORE = -1e30
LOG2E = 1.4426950408889634


def from_partner(value, axis):
    return lax.ppermute(value, axis, [(i, i ^ 1) for i in range(lax.axis_size(axis))])


def turn(x, cosine, sine):
    x = x.astype(jnp.float32)
    return (x * cosine + pltpu.roll(x, HD // 2, 1) * sine).astype(jnp.bfloat16)


def attend(rows, q_own, q_peer, k_own, v_own, kc, vc, cos_ref, sin_ref, bias, fresh_bias, o_ref, lse_ref):
    c = LOG2E / math.sqrt(HD)
    parts = []
    for g in range(GROUP):
        cut = slice(g * HD, (g + 1) * HD)
        parts.append(turn(q_own[:, cut], cos_ref[:rows], sin_ref[:rows]))
        parts.append(turn(q_peer[:, cut], cos_ref[rows:], sin_ref[rows:]))
    q = jnp.concatenate(parts, axis=0)
    keys = turn(k_own[...], cos_ref[:rows], sin_ref[:rows])
    dims = (((1,), (1,)), ((), ()))
    s = lax.dot_general(q, keys, dims, preferred_element_type=jnp.float32) * c
    s = s + jnp.concatenate([fresh_bias[...]] * GROUP, axis=0)
    m = jnp.max(s, axis=1, keepdims=True)
    p = jnp.exp2(s - m)
    l = jnp.sum(p, axis=1, keepdims=True)
    o = jnp.dot(p.astype(jnp.bfloat16), v_own[...], preferred_element_type=jnp.float32)
    for first in range(0, kc.shape[0], CHUNK):
        cut = slice(first, first + CHUNK)
        s = lax.dot_general(q, kc[cut], dims, preferred_element_type=jnp.float32) * c + bias[:, cut]
        top = jnp.maximum(m, jnp.max(s, axis=1, keepdims=True))
        factor = jnp.exp2(m - top)
        m = top
        p = jnp.exp2(s - m)
        l = l * factor + jnp.sum(p, axis=1, keepdims=True)
        o = o * factor + jnp.dot(p.astype(jnp.bfloat16), vc[cut], preferred_element_type=jnp.float32)
    o = (o / l).astype(jnp.bfloat16)
    lse = m + jnp.log2(l)
    for g in range(GROUP):
        o_ref[:, g * HD : (g + 1) * HD] = o[g * 2 * rows : (g + 1) * 2 * rows]
        lse_ref[:, g : g + 1] = lse[g * 2 * rows : (g + 1) * 2 * rows]


def tables(q_new, k_cache, lengths, page_table):
    rows = q_new.shape[0]
    pages, page_rows = k_cache.shape[0], k_cache.shape[1]
    device_row = lax.axis_index("req")
    parity = device_row % 2
    request = device_row // 2
    length = lengths[request]
    token = (jnp.arange(2 * rows) + parity * rows) % (2 * rows)
    inverse = 1.0 / ROPE_BASE ** (jnp.arange(0, HD, 2).astype(jnp.float32) / HD)
    angles = (length + token).astype(jnp.float32)[:, None] * inverse[None, :]
    cosine = jnp.concatenate([jnp.cos(angles)] * 2, axis=-1)
    sine = jnp.sin(angles)
    sine = jnp.concatenate([-sine, sine], axis=-1)
    slot = device_row * pages + jnp.arange(pages)
    same = page_table[request][None, :] == slot[:, None]
    logical = jnp.max(jnp.where(same, jnp.arange(page_table.shape[1])[None, :], -1), axis=1)
    place = logical[:, None] * page_rows + jnp.arange(page_rows)[None, :]
    usable = (logical >= 0)[:, None] & (place < length)
    bias = jnp.where(usable, 0.0, FLOOR_SCORE).astype(jnp.float32).reshape(1, pages * page_rows)
    fresh = token[None, :rows] <= token[:, None]
    fresh_bias = jnp.where(fresh, 0.0, FLOOR_SCORE).astype(jnp.float32)
    return cosine, sine, bias, fresh_bias


def shards(q_new, k_new, v_new, k_cache, v_cache, lengths, page_table, w_out):
    rows = q_new.shape[0]
    heads = k_new.shape[1] // HD
    keys = k_cache.shape[0] * k_cache.shape[1]
    peer_q = from_partner(q_new, "req")
    cosine, sine, bias, fresh_bias = tables(q_new, k_cache, lengths, page_table)
    wide = GROUP * HD
    whole = lambda shape: pl.BlockSpec(shape, lambda h: (0, 0))
    by_head = lambda n, w: pl.BlockSpec((n, w), lambda h: (0, h))
    o, lse = pl.pallas_call(
        lambda *refs: attend(rows, *refs),
        grid=(heads,),
        in_specs=[
            by_head(rows, wide),
            by_head(rows, wide),
            by_head(rows, HD),
            by_head(rows, HD),
            by_head(keys, HD),
            by_head(keys, HD),
            whole((2 * rows, HD)),
            whole((2 * rows, HD)),
            whole((1, keys)),
            whole((2 * rows, rows)),
        ],
        out_specs=[by_head(2 * rows, wide), by_head(2 * rows, HD)],
        out_shape=[
            jax.ShapeDtypeStruct((2 * rows, heads * wide), jnp.bfloat16),
            jax.ShapeDtypeStruct((2 * rows, heads * HD), jnp.float32),
        ],
        compiler_params=pltpu.CompilerParams(vmem_limit_bytes=48 * 2**20),
    )(
        q_new,
        peer_q,
        k_new,
        v_new,
        k_cache.reshape(keys, heads * HD),
        v_cache.reshape(keys, heads * HD),
        cosine,
        sine,
        bias,
        fresh_bias,
    )
    lse = lse.reshape(2 * rows, heads, HD)[:, :, :GROUP].reshape(2 * rows, heads * GROUP)
    other_o = from_partner(o[rows:], "req")
    other_lse = from_partner(lse[rows:], "req")
    share = 1.0 / (1.0 + jnp.exp2(other_lse - lse[:rows]))
    share = share[:, :, None]
    mine = o[:rows].reshape(rows, heads * GROUP, HD).astype(jnp.float32)
    theirs = other_o.reshape(rows, heads * GROUP, HD).astype(jnp.float32)
    attention = (mine * share + theirs * (1.0 - share)).astype(jnp.bfloat16)
    gathered = lax.all_gather(attention.reshape(rows, heads * wide), "req", axis=0, tiled=True)
    part = lax.dot_general(
        gathered, w_out, (((1,), (1,)), ((), ())), preferred_element_type=jnp.float32
    ).astype(jnp.bfloat16)
    part = lax.all_to_all(part, "req", split_axis=0, concat_axis=1, tiled=True)
    return lax.psum(part, "tp")


def solution(mesh):
    in_specs = (
        P("req", "tp"),
        P("req", "tp"),
        P("req", "tp"),
        P("req", None, "tp"),
        P("req", None, "tp"),
        P(),
        P(),
        P("req", "tp"),
    )
    return jax.shard_map(
        shards, mesh=mesh, in_specs=in_specs, out_specs=P("req", None), check_vma=False
    )
```

```python
import math

import jax
import jax.numpy as jnp
from jax import lax
from jax.experimental import pallas as pl
from jax.experimental.pallas import tpu as pltpu
from jax.sharding import PartitionSpec as P

HD = 128
GROUP = 5
CHUNK = 512
ROPE_BASE = 1000000.0
FLOOR_SCORE = -1e30
LOG2E = 1.4426950408889634


def from_partner(value, axis):
    return lax.ppermute(value, axis, [(i, i ^ 1) for i in range(lax.axis_size(axis))])


def turn(x, cosine, sine):
    x = x.astype(jnp.float32)
    return (x * cosine + pltpu.roll(x, HD // 2, 1) * sine).astype(jnp.bfloat16)


def attend(rows, q_own, q_peer, k_own, v_own, kc, vc, cos_ref, sin_ref, bias, fresh_bias, o_ref, lse_ref):
    c = LOG2E / math.sqrt(HD)
    parts = []
    for g in range(GROUP):
        cut = slice(g * HD, (g + 1) * HD)
        parts.append(turn(q_own[:, cut], cos_ref[:rows], sin_ref[:rows]))
        parts.append(turn(q_peer[:, cut], cos_ref[rows:], sin_ref[rows:]))
    q = jnp.concatenate(parts, axis=0)
    keys = turn(k_own[...], cos_ref[:rows], sin_ref[:rows])
    dims = (((1,), (1,)), ((), ()))
    s = lax.dot_general(q, keys, dims, preferred_element_type=jnp.float32) * c
    s = s + jnp.concatenate([fresh_bias[...]] * GROUP, axis=0)
    m = jnp.max(s, axis=1, keepdims=True)
    p = jnp.exp2(s - m)
    l = jnp.sum(p, axis=1, keepdims=True)
    o = jnp.dot(p.astype(jnp.bfloat16), v_own[...], preferred_element_type=jnp.float32)
    for first in range(0, kc.shape[0], CHUNK):
        cut = slice(first, first + CHUNK)
        s = lax.dot_general(q, kc[cut], dims, preferred_element_type=jnp.float32) * c + bias[:, cut]
        top = jnp.maximum(m, jnp.max(s, axis=1, keepdims=True))
        factor = jnp.exp2(m - top)
        m = top
        p = jnp.exp2(s - m)
        l = l * factor + jnp.sum(p, axis=1, keepdims=True)
        o = o * factor + jnp.dot(p.astype(jnp.bfloat16), vc[cut], preferred_element_type=jnp.float32)
    o = (o / l).astype(jnp.bfloat16)
    lse = m + jnp.log2(l)
    for g in range(GROUP):
        o_ref[:, g * HD : (g + 1) * HD] = o[g * 2 * rows : (g + 1) * 2 * rows]
        lse_ref[:, g : g + 1] = lse[g * 2 * rows : (g + 1) * 2 * rows]


def project_kernel(n, att, w, out, gat, part, ybuf, red, ring_s, ring_r, core_s, core_r, y_s, y_r, sc_s, sc_r, f_s, f_r):
    chips = n // 2
    side = chips // 2
    me = lax.axis_index("req")
    t = lax.axis_index("tp")
    core = me % 2
    chip = me // 2
    column = chip % 2
    place = (1 - column) * (chip // 2) + column * (chips - 1 - chip // 2)

    def chip_at(offset):
        pos = (place + offset + chips) % chips
        far = pos // side
        return (1 - far) * 2 * pos + far * (2 * (chips - 1 - pos) + 1)

    peer = me + 1 - 2 * core
    barrier = pltpu.get_barrier_semaphore()
    for k in range(1, n):
        pl.semaphore_signal(
            barrier, inc=1, device_id=((me + k) % n, t), device_id_type=pl.DeviceIdType.MESH
        )
    pl.semaphore_signal(barrier, inc=1, device_id=(me, 1 - t), device_id_type=pl.DeviceIdType.MESH)
    pl.semaphore_wait(barrier, n)

    def remote(src, dst, s, r, row, col):
        return pltpu.make_async_remote_copy(
            src_ref=src, dst_ref=dst, send_sem=s, recv_sem=r,
            device_id=(row, col), device_id_type=pl.DeviceIdType.MESH,
        )

    gat[me] = att[...]
    left = chip_at(-1) * 2 + core
    right = chip_at(1) * 2 + core
    steps_up = chips // 2
    steps_down = chips - 1 - steps_up

    def ring(d, j, to):
        block = chip_at(j if d == 0 else -j) * 2 + core
        slot = d * chips + j
        return remote(gat.at[block], gat.at[block], ring_s.at[slot], ring_r.at[slot], to, t)

    def cross(offset):
        block = chip_at(offset) * 2 + core
        slot = offset % chips
        return remote(gat.at[block], gat.at[block], core_s.at[slot], core_r.at[slot], peer, t)

    sent = []

    def start(copy):
        copy.start()
        sent.append(copy)

    start(ring(0, 0, left))
    start(ring(1, 0, right))
    start(cross(0))

    def trade(offset):
        c = chip_at(offset)
        slot = offset % chips
        return remote(part.at[c, 1 - t], ybuf.at[c], y_s.at[slot], y_r.at[slot], me, 1 - t)

    def multiply(offset):
        c = chip_at(offset)
        cross(offset).wait_recv()
        rows = gat.shape[1]
        half = rows // 2
        for k in range(2):
            got = lax.dot_general(
                gat[2 * c + k], w[...], (((1,), (1,)), ((), ())), preferred_element_type=jnp.float32
            ).astype(jnp.bfloat16)
            part[c, 0, k] = got[:half]
            part[c, 1, k] = got[half:]
        start(trade(offset))

    def scatter(offset, k):
        slot = (offset % chips) * 2 + k
        c = chip_at(offset)
        dev = 2 * c + (core + k) % 2
        return remote(red.at[c, (core + k) % 2], out.at[me, t], sc_s.at[slot], sc_r.at[slot], dev, t)

    def reduce(offset):
        c = chip_at(offset)
        trade(offset).wait_recv()
        total = part[c, t].astype(jnp.float32) + ybuf[c].astype(jnp.float32)
        red[c] = total.astype(jnp.bfloat16)
        if offset == 0:
            out[me, t] = red[c, core]
        else:
            start(scatter(offset, 0))
        start(scatter(offset, 1))

    def forward(offset, k):
        slot = (offset % chips) * 2 + k
        dev = chip_at(offset) * 2 + (core + k) % 2
        return remote(out.at[dev, t], out.at[dev, t], f_s.at[slot], f_r.at[slot], me, 1 - t)

    def landed(offset, k):
        slot = ((-offset) % chips) * 2 + k
        dev = chip_at(offset) * 2 + (core + k) % 2
        return remote(red.at[0, 0], out.at[dev, t], sc_s.at[slot], sc_r.at[slot], dev, t)

    def collect(offset):
        for k in range(2):
            if offset != 0 or k == 1:
                landed(offset, k).wait_recv()
            start(forward(offset, k))

    order = [0]
    for j in range(1, steps_up + 1):
        order.append(j)
        if j <= steps_down:
            order.append(-j)
    done = 0
    for j in range(1, steps_up + 1):
        remote(gat.at[0], gat.at[chip_at(j) * 2 + core], ring_s.at[j - 1], ring_r.at[j - 1], left, t).wait_recv()
        if j < steps_up:
            start(ring(0, j, left))
        start(cross(j))
        if j <= steps_down:
            slot = chips + j - 1
            remote(gat.at[0], gat.at[chip_at(-j) * 2 + core], ring_s.at[slot], ring_r.at[slot], right, t).wait_recv()
            if j < steps_down:
                start(ring(1, j, right))
            start(cross(-j))
        ready = 1 if j == 1 else 2 * j - 1
        while done < min(ready, len(order)):
            multiply(order[done])
            if done >= 1:
                reduce(order[done - 1])
            done += 1
    while done < len(order):
        multiply(order[done])
        reduce(order[done - 1])
        done += 1
    reduce(order[-1])
    for offset in order:
        collect(offset)
    for offset in order:
        for k in range(2):
            dev = chip_at(offset) * 2 + (core + k) % 2
            slot = (offset % chips) * 2 + k
            remote(red.at[0, 0], out.at[dev, 1 - t], f_s.at[slot], f_r.at[slot], me, 1 - t).wait_recv()
    for copy in sent:
        copy.wait_send()


def project(attention, w_out):
    n = lax.axis_size("req")
    rows, deep = attention.shape
    cols = w_out.shape[0]
    chips = n // 2
    half = rows // 2
    dma = pltpu.SemaphoreType.DMA
    vmem = pl.BlockSpec(memory_space=pltpu.VMEM)
    out = pl.pallas_call(
        lambda *refs: project_kernel(n, *refs),
        in_specs=[vmem, vmem],
        out_specs=vmem,
        out_shape=jax.ShapeDtypeStruct((n, 2, half, cols), jnp.bfloat16),
        scratch_shapes=[
            pltpu.VMEM((n, rows, deep), jnp.bfloat16),
            pltpu.VMEM((chips, 2, 2, half, cols), jnp.bfloat16),
            pltpu.VMEM((chips, 2, half, cols), jnp.bfloat16),
            pltpu.VMEM((chips, 2, half, cols), jnp.bfloat16),
            dma((2 * chips,)),
            dma((2 * chips,)),
            dma((chips,)),
            dma((chips,)),
            dma((chips,)),
            dma((chips,)),
            dma((n,)),
            dma((n,)),
            dma((n,)),
            dma((n,)),
        ],
        compiler_params=pltpu.CompilerParams(
            collective_id=0, has_side_effects=True, vmem_limit_bytes=40 * 2**20
        ),
    )(attention, w_out)
    return jnp.transpose(out.reshape(n, rows, cols), (1, 0, 2)).reshape(rows, n * cols)


def tables(q_new, k_cache, lengths, page_table):
    rows = q_new.shape[0]
    pages, page_rows = k_cache.shape[0], k_cache.shape[1]
    device_row = lax.axis_index("req")
    parity = device_row % 2
    request = device_row // 2
    length = lengths[request]
    token = (jnp.arange(2 * rows) + parity * rows) % (2 * rows)
    inverse = 1.0 / ROPE_BASE ** (jnp.arange(0, HD, 2).astype(jnp.float32) / HD)
    angles = (length + token).astype(jnp.float32)[:, None] * inverse[None, :]
    cosine = jnp.concatenate([jnp.cos(angles)] * 2, axis=-1)
    sine = jnp.sin(angles)
    sine = jnp.concatenate([-sine, sine], axis=-1)
    slot = device_row * pages + jnp.arange(pages)
    same = page_table[request][None, :] == slot[:, None]
    logical = jnp.max(jnp.where(same, jnp.arange(page_table.shape[1])[None, :], -1), axis=1)
    place = logical[:, None] * page_rows + jnp.arange(page_rows)[None, :]
    usable = (logical >= 0)[:, None] & (place < length)
    bias = jnp.where(usable, 0.0, FLOOR_SCORE).astype(jnp.float32).reshape(1, pages * page_rows)
    fresh = token[None, :rows] <= token[:, None]
    fresh_bias = jnp.where(fresh, 0.0, FLOOR_SCORE).astype(jnp.float32)
    return cosine, sine, bias, fresh_bias


def shards(q_new, k_new, v_new, k_cache, v_cache, lengths, page_table, w_out):
    rows = q_new.shape[0]
    heads = k_new.shape[1] // HD
    keys = k_cache.shape[0] * k_cache.shape[1]
    peer_q = from_partner(q_new, "req")
    cosine, sine, bias, fresh_bias = tables(q_new, k_cache, lengths, page_table)
    wide = GROUP * HD
    whole = lambda shape: pl.BlockSpec(shape, lambda h: (0, 0))
    by_head = lambda n, w: pl.BlockSpec((n, w), lambda h: (0, h))
    o, lse = pl.pallas_call(
        lambda *refs: attend(rows, *refs),
        grid=(heads,),
        in_specs=[
            by_head(rows, wide),
            by_head(rows, wide),
            by_head(rows, HD),
            by_head(rows, HD),
            by_head(keys, HD),
            by_head(keys, HD),
            whole((2 * rows, HD)),
            whole((2 * rows, HD)),
            whole((1, keys)),
            whole((2 * rows, rows)),
        ],
        out_specs=[by_head(2 * rows, wide), by_head(2 * rows, HD)],
        out_shape=[
            jax.ShapeDtypeStruct((2 * rows, heads * wide), jnp.bfloat16),
            jax.ShapeDtypeStruct((2 * rows, heads * HD), jnp.float32),
        ],
        compiler_params=pltpu.CompilerParams(vmem_limit_bytes=48 * 2**20),
    )(
        q_new,
        peer_q,
        k_new,
        v_new,
        k_cache.reshape(keys, heads * HD),
        v_cache.reshape(keys, heads * HD),
        cosine,
        sine,
        bias,
        fresh_bias,
    )
    lse = lse.reshape(2 * rows, heads, HD)[:, :, :GROUP].reshape(2 * rows, heads * GROUP)
    other_o = from_partner(o[rows:], "req")
    other_lse = from_partner(lse[rows:], "req")
    share = 1.0 / (1.0 + jnp.exp2(other_lse - lse[:rows]))
    share = share[:, :, None]
    mine = o[:rows].reshape(rows, heads * GROUP, HD).astype(jnp.float32)
    theirs = other_o.reshape(rows, heads * GROUP, HD).astype(jnp.float32)
    attention = (mine * share + theirs * (1.0 - share)).astype(jnp.bfloat16)
    attention = attention.reshape(rows, heads * wide)
    if lax.axis_size("tp") == 2 and rows % 32 == 0 and lax.axis_size("req") % 4 == 0:
        return project(attention, w_out)
    gathered = lax.all_gather(attention, "req", axis=0, tiled=True)
    part = lax.dot_general(
        gathered, w_out, (((1,), (1,)), ((), ())), preferred_element_type=jnp.float32
    ).astype(jnp.bfloat16)
    part = lax.all_to_all(part, "req", split_axis=0, concat_axis=1, tiled=True)
    return lax.psum(part, "tp")


def solution(mesh):
    in_specs = (
        P("req", "tp"),
        P("req", "tp"),
        P("req", "tp"),
        P("req", None, "tp"),
        P("req", None, "tp"),
        P(),
        P(),
        P("req", "tp"),
    )
    return jax.shard_map(
        shards, mesh=mesh, in_specs=in_specs, out_specs=P("req", None), check_vma=False
    )
```

```python
import math

import jax
import jax.numpy as jnp
from jax import lax
from jax.experimental import pallas as pl
from jax.experimental.pallas import tpu as pltpu
from jax.sharding import PartitionSpec as P

HD = 128
GROUP = 5
CHUNK = 512
ROPE_BASE = 1000000.0
FLOOR_SCORE = -1e30
LOG2E = 1.4426950408889634


def from_partner(value, axis):
    return lax.ppermute(value, axis, [(i, i ^ 1) for i in range(lax.axis_size(axis))])


def turn(x, cosine, sine):
    x = x.astype(jnp.float32)
    return (x * cosine + pltpu.roll(x, HD // 2, 1) * sine).astype(jnp.bfloat16)


def attend(rows, q_own, q_peer, k_own, v_own, kc, vc, cos_ref, sin_ref, bias, fresh_bias, o_ref, lse_ref):
    c = LOG2E / math.sqrt(HD)
    parts = []
    for g in range(GROUP):
        cut = slice(g * HD, (g + 1) * HD)
        parts.append(turn(q_own[:, cut], cos_ref[:rows], sin_ref[:rows]))
        parts.append(turn(q_peer[:, cut], cos_ref[rows:], sin_ref[rows:]))
    q = jnp.concatenate(parts, axis=0)
    keys = turn(k_own[...], cos_ref[:rows], sin_ref[:rows])
    dims = (((1,), (1,)), ((), ()))
    s = lax.dot_general(q, keys, dims, preferred_element_type=jnp.float32) * c
    s = s + jnp.concatenate([fresh_bias[...]] * GROUP, axis=0)
    m = jnp.max(s, axis=1, keepdims=True)
    p = jnp.exp2(s - m)
    l = jnp.sum(p, axis=1, keepdims=True)
    o = jnp.dot(p.astype(jnp.bfloat16), v_own[...], preferred_element_type=jnp.float32)
    for first in range(0, kc.shape[0], CHUNK):
        cut = slice(first, first + CHUNK)
        s = lax.dot_general(q, kc[cut], dims, preferred_element_type=jnp.float32) * c + bias[:, cut]
        top = jnp.maximum(m, jnp.max(s, axis=1, keepdims=True))
        factor = jnp.exp2(m - top)
        m = top
        p = jnp.exp2(s - m)
        l = l * factor + jnp.sum(p, axis=1, keepdims=True)
        o = o * factor + jnp.dot(p.astype(jnp.bfloat16), vc[cut], preferred_element_type=jnp.float32)
    o = (o / l).astype(jnp.bfloat16)
    lse = m + jnp.log2(l)
    for g in range(GROUP):
        o_ref[:, g * HD : (g + 1) * HD] = o[g * 2 * rows : (g + 1) * 2 * rows]
        lse_ref[:, g : g + 1] = lse[g * 2 * rows : (g + 1) * 2 * rows]


def project_kernel(n, att, w, out, gat, part, ybuf, red, ring_s, ring_r, core_s, core_r, y_s, y_r, sc_s, sc_r, f_s, f_r):
    chips = n // 2
    side = chips // 2
    me = lax.axis_index("req")
    t = lax.axis_index("tp")
    core = me % 2
    chip = me // 2
    column = chip % 2
    place = (1 - column) * (chip // 2) + column * (chips - 1 - chip // 2)

    def chip_at(offset):
        pos = (place + offset + chips) % chips
        far = pos // side
        return (1 - far) * 2 * pos + far * (2 * (chips - 1 - pos) + 1)

    peer = me + 1 - 2 * core
    barrier = pltpu.get_barrier_semaphore()
    for k in range(1, n):
        pl.semaphore_signal(
            barrier, inc=1, device_id=((me + k) % n, t), device_id_type=pl.DeviceIdType.MESH
        )
    pl.semaphore_signal(barrier, inc=1, device_id=(me, 1 - t), device_id_type=pl.DeviceIdType.MESH)
    pl.semaphore_wait(barrier, n)

    def remote(src, dst, s, r, row, col):
        return pltpu.make_async_remote_copy(
            src_ref=src, dst_ref=dst, send_sem=s, recv_sem=r,
            device_id=(row, col), device_id_type=pl.DeviceIdType.MESH,
        )

    gat[me] = att[...]
    left = chip_at(-1) * 2 + core
    right = chip_at(1) * 2 + core
    steps_up = chips // 2
    steps_down = chips - 1 - steps_up

    def ring(d, j, to):
        block = chip_at(j if d == 0 else -j) * 2 + core
        slot = d * chips + j
        return remote(gat.at[block], gat.at[block], ring_s.at[slot], ring_r.at[slot], to, t)

    def cross(offset):
        block = chip_at(offset) * 2 + core
        slot = offset % chips
        return remote(gat.at[block], gat.at[block], core_s.at[slot], core_r.at[slot], peer, t)

    sent = []

    def start(copy):
        copy.start()
        sent.append(copy)

    start(ring(0, 0, left))
    start(ring(1, 0, right))
    start(cross(0))

    def trade(offset):
        c = chip_at(offset)
        slot = offset % chips
        return remote(part.at[c, 1 - t], ybuf.at[c], y_s.at[slot], y_r.at[slot], me, 1 - t)

    def multiply(offset):
        c = chip_at(offset)
        cross(offset).wait_recv()
        rows = gat.shape[1]
        half = rows // 2
        both = gat[pl.ds(2 * c, 2)].reshape(2 * rows, gat.shape[2])
        got = lax.dot_general(
            both, w[...], (((1,), (1,)), ((), ())), preferred_element_type=jnp.float32
        ).astype(jnp.bfloat16)
        for k in range(2):
            part[c, 0, k] = got[k * rows : k * rows + half]
            part[c, 1, k] = got[k * rows + half : (k + 1) * rows]
        start(trade(offset))

    def scatter(offset, k):
        slot = (offset % chips) * 2 + k
        c = chip_at(offset)
        dev = 2 * c + (core + k) % 2
        return remote(red.at[c, (core + k) % 2], out.at[me, t], sc_s.at[slot], sc_r.at[slot], dev, t)

    def reduce(offset):
        c = chip_at(offset)
        trade(offset).wait_recv()
        total = part[c, t].astype(jnp.float32) + ybuf[c].astype(jnp.float32)
        red[c] = total.astype(jnp.bfloat16)
        if offset == 0:
            out[me, t] = red[c, core]
        else:
            start(scatter(offset, 0))
        start(scatter(offset, 1))

    def forward(offset, k):
        slot = (offset % chips) * 2 + k
        dev = chip_at(offset) * 2 + (core + k) % 2
        return remote(out.at[dev, t], out.at[dev, t], f_s.at[slot], f_r.at[slot], me, 1 - t)

    def landed(offset, k):
        slot = ((-offset) % chips) * 2 + k
        dev = chip_at(offset) * 2 + (core + k) % 2
        return remote(red.at[0, 0], out.at[dev, t], sc_s.at[slot], sc_r.at[slot], dev, t)

    def collect(offset):
        for k in range(2):
            if offset != 0 or k == 1:
                landed(offset, k).wait_recv()
            start(forward(offset, k))

    order = [0]
    for j in range(1, steps_up + 1):
        order.append(j)
        if j <= steps_down:
            order.append(-j)
    done = 0
    for j in range(1, steps_up + 1):
        remote(gat.at[0], gat.at[chip_at(j) * 2 + core], ring_s.at[j - 1], ring_r.at[j - 1], left, t).wait_recv()
        if j < steps_up:
            start(ring(0, j, left))
        start(cross(j))
        if j <= steps_down:
            slot = chips + j - 1
            remote(gat.at[0], gat.at[chip_at(-j) * 2 + core], ring_s.at[slot], ring_r.at[slot], right, t).wait_recv()
            if j < steps_down:
                start(ring(1, j, right))
            start(cross(-j))
        ready = 1 if j == 1 else 2 * j - 1
        while done < min(ready, len(order)):
            multiply(order[done])
            if done >= 1:
                reduce(order[done - 1])
            if done >= 4:
                collect(order[done - 4])
            done += 1
    while done < len(order):
        multiply(order[done])
        reduce(order[done - 1])
        if done >= 4:
            collect(order[done - 4])
        done += 1
    reduce(order[-1])
    for offset in order[max(0, len(order) - 4) :]:
        collect(offset)
    for offset in order:
        for k in range(2):
            dev = chip_at(offset) * 2 + (core + k) % 2
            slot = (offset % chips) * 2 + k
            remote(red.at[0, 0], out.at[dev, 1 - t], f_s.at[slot], f_r.at[slot], me, 1 - t).wait_recv()
    for copy in sent:
        copy.wait_send()


def project(attention, w_out):
    n = lax.axis_size("req")
    rows, deep = attention.shape
    cols = w_out.shape[0]
    chips = n // 2
    half = rows // 2
    dma = pltpu.SemaphoreType.DMA
    vmem = pl.BlockSpec(memory_space=pltpu.VMEM)
    out = pl.pallas_call(
        lambda *refs: project_kernel(n, *refs),
        in_specs=[vmem, vmem],
        out_specs=vmem,
        out_shape=jax.ShapeDtypeStruct((n, 2, half, cols), jnp.bfloat16),
        scratch_shapes=[
            pltpu.VMEM((n, rows, deep), jnp.bfloat16),
            pltpu.VMEM((chips, 2, 2, half, cols), jnp.bfloat16),
            pltpu.VMEM((chips, 2, half, cols), jnp.bfloat16),
            pltpu.VMEM((chips, 2, half, cols), jnp.bfloat16),
            dma((2 * chips,)),
            dma((2 * chips,)),
            dma((chips,)),
            dma((chips,)),
            dma((chips,)),
            dma((chips,)),
            dma((n,)),
            dma((n,)),
            dma((n,)),
            dma((n,)),
        ],
        compiler_params=pltpu.CompilerParams(
            collective_id=0, has_side_effects=True, vmem_limit_bytes=40 * 2**20
        ),
    )(attention, w_out)
    return jnp.transpose(out.reshape(n, rows, cols), (1, 0, 2)).reshape(rows, n * cols)


def tables(q_new, k_cache, lengths, page_table):
    rows = q_new.shape[0]
    pages, page_rows = k_cache.shape[0], k_cache.shape[1]
    device_row = lax.axis_index("req")
    parity = device_row % 2
    request = device_row // 2
    length = lengths[request]
    token = (jnp.arange(2 * rows) + parity * rows) % (2 * rows)
    inverse = 1.0 / ROPE_BASE ** (jnp.arange(0, HD, 2).astype(jnp.float32) / HD)
    angles = (length + token).astype(jnp.float32)[:, None] * inverse[None, :]
    cosine = jnp.concatenate([jnp.cos(angles)] * 2, axis=-1)
    sine = jnp.sin(angles)
    sine = jnp.concatenate([-sine, sine], axis=-1)
    slot = device_row * pages + jnp.arange(pages)
    same = page_table[request][None, :] == slot[:, None]
    logical = jnp.max(jnp.where(same, jnp.arange(page_table.shape[1])[None, :], -1), axis=1)
    place = logical[:, None] * page_rows + jnp.arange(page_rows)[None, :]
    usable = (logical >= 0)[:, None] & (place < length)
    bias = jnp.where(usable, 0.0, FLOOR_SCORE).astype(jnp.float32).reshape(1, pages * page_rows)
    fresh = token[None, :rows] <= token[:, None]
    fresh_bias = jnp.where(fresh, 0.0, FLOOR_SCORE).astype(jnp.float32)
    return cosine, sine, bias, fresh_bias


def shards(q_new, k_new, v_new, k_cache, v_cache, lengths, page_table, w_out):
    rows = q_new.shape[0]
    heads = k_new.shape[1] // HD
    keys = k_cache.shape[0] * k_cache.shape[1]
    peer_q = from_partner(q_new, "req")
    cosine, sine, bias, fresh_bias = tables(q_new, k_cache, lengths, page_table)
    wide = GROUP * HD
    whole = lambda shape: pl.BlockSpec(shape, lambda h: (0, 0))
    by_head = lambda n, w: pl.BlockSpec((n, w), lambda h: (0, h))
    o, lse = pl.pallas_call(
        lambda *refs: attend(rows, *refs),
        grid=(heads,),
        in_specs=[
            by_head(rows, wide),
            by_head(rows, wide),
            by_head(rows, HD),
            by_head(rows, HD),
            by_head(keys, HD),
            by_head(keys, HD),
            whole((2 * rows, HD)),
            whole((2 * rows, HD)),
            whole((1, keys)),
            whole((2 * rows, rows)),
        ],
        out_specs=[by_head(2 * rows, wide), by_head(2 * rows, HD)],
        out_shape=[
            jax.ShapeDtypeStruct((2 * rows, heads * wide), jnp.bfloat16),
            jax.ShapeDtypeStruct((2 * rows, heads * HD), jnp.float32),
        ],
        compiler_params=pltpu.CompilerParams(vmem_limit_bytes=60 * 2**20),
    )(
        q_new,
        peer_q,
        k_new,
        v_new,
        k_cache.reshape(keys, heads * HD),
        v_cache.reshape(keys, heads * HD),
        cosine,
        sine,
        bias,
        fresh_bias,
    )
    lse = lse.reshape(2 * rows, heads, HD)[:, :, :GROUP].reshape(2 * rows, heads * GROUP)
    other_o = from_partner(o[rows:], "req")
    other_lse = from_partner(lse[rows:], "req")
    share = 1.0 / (1.0 + jnp.exp2(other_lse - lse[:rows]))
    share = share[:, :, None]
    mine = o[:rows].reshape(rows, heads * GROUP, HD).astype(jnp.float32)
    theirs = other_o.reshape(rows, heads * GROUP, HD).astype(jnp.float32)
    attention = (mine * share + theirs * (1.0 - share)).astype(jnp.bfloat16)
    attention = attention.reshape(rows, heads * wide)
    if lax.axis_size("tp") == 2 and rows % 32 == 0 and lax.axis_size("req") % 4 == 0:
        return project(attention, w_out)
    gathered = lax.all_gather(attention, "req", axis=0, tiled=True)
    part = lax.dot_general(
        gathered, w_out, (((1,), (1,)), ((), ())), preferred_element_type=jnp.float32
    ).astype(jnp.bfloat16)
    part = lax.all_to_all(part, "req", split_axis=0, concat_axis=1, tiled=True)
    return lax.psum(part, "tp")


def solution(mesh):
    in_specs = (
        P("req", "tp"),
        P("req", "tp"),
        P("req", "tp"),
        P("req", None, "tp"),
        P("req", None, "tp"),
        P(),
        P(),
        P("req", "tp"),
    )
    return jax.shard_map(
        shards, mesh=mesh, in_specs=in_specs, out_specs=P("req", None), check_vma=False
    )
```
